512 devices in a mesh: section: 4 (over y), ctx: 32 (over x, z_lo), tp: 4 (over z_hi, core).
Axes of the slice: x: 4, y: 4, z: 16 (z_hi: 2, z_lo: 8; z = z_hi * 8 + z_lo), core: 2. Of those that a mesh axis runs over, the one named last changes fastest.
Arguments:
- queries: bfloat16 [4, 6144, 8192], P('section', 'ctx', 'tp'), may hold values from -180 to 180
- keys: bfloat16 [4, 6144, 1024], P('section', 'ctx', 'tp'), may hold values from -6 to 6
- values: bfloat16 [4, 6144, 1024], P('section', 'ctx', 'tp'), may hold values from -6 to 6
- modality: int32 [4, 6144], P('section', 'ctx'), may hold values from 0 to 1
- query_gain: float32 [2, 8192], P(None, 'tp'), may hold values from 0.5 to 1.5
- tower_key_gain: float32 [2, 1024], P(None, 'tp'), may hold values from 0.5 to 1.5
- doc_lengths: int32 [4, 16], P('section'), may hold values from 1 to 3840, 6144 in all within a row
Outputs:
- handed: bfloat16 [4, 6144, 8192], P('section', 'ctx', 'tp')
The draws below stay inside these ranges and needn't reach their ends.
Inputs may be any that keep to these rules, and one draw needn't show every extreme that they name: `doc_lengths`: each row sums to 6144; its longest document has exactly 3840 tokens.
All inputs are finite; a program needn't handle non-finite values.
Results may differ from the reference program's by a relative error of at most 0.012.
The reference program's roundings to bfloat16 on the way count: a program that leaves them out, or rounds other values in their place, can miss the bound.
Values may be sent and summed in bfloat16 or wider, within the bound.
A program may use at most 64 MiB of HBM per device.

```python
import math
import jax
import jax.numpy as jnp
import numpy as np
from jax import lax

QUERY_HEADS = 64
KEY_VALUE_HEADS = 8
HEAD_SIZE = 128
DOCS = 16
SEQUENCE_TOKENS = 6144
RELAY_SECTIONS = 4


def initial_keys(key):
    return jnp.clip(jax.random.normal(key, (RELAY_SECTIONS, SEQUENCE_TOKENS, KEY_VALUE_HEADS * HEAD_SIZE), jnp.float32), -6.0, 6.0)


def draw_keys(key, part):
    return initial_keys(key).astype(jnp.bfloat16)


def draw_queries(key, part):
    own_key = jax.random.fold_in(key, 3)
    drawn = jnp.clip(jax.random.normal(own_key, (RELAY_SECTIONS, SEQUENCE_TOKENS, QUERY_HEADS * HEAD_SIZE), jnp.float32), -6.0, 6.0)
    return drawn.astype(jnp.bfloat16)


def plant(entries, rng, smallest, top_value):
    shape = entries.shape
    spot = [jax.random.randint(jax.random.fold_in(rng, axis), (), 0, shape[axis]) for axis in range(len(shape))]
    entries = entries.at[tuple(spot)].set(smallest)
    longest = shape.index(max(shape))
    spot[longest] = (spot[longest] + 1) % shape[longest]
    return entries.at[tuple(spot)].set(top_value)


def block_scale(key, dims, shards, smallest, largest):
    factor_of = 1.0
    for position, shards_of in shards:
        heights = jax.random.uniform(jax.random.fold_in(jax.random.fold_in(key, 6), position), (shards_of,), jnp.float32, smallest / len(shards), largest / len(shards))
        factor_of = factor_of * jnp.repeat(jnp.exp(heights), dims[position] // shards_of).reshape((-1,) + (1,) * (len(dims) - 1 - position))
    return factor_of


def profile(count, total, reach, slope):
    loads = [(1 << 20) // math.isqrt(standing ** slope) + 1 for standing in range(2, count + 1)]
    rest, given = total - reach - (count - 1), [1] * (count - 1)
    while rest > 0:
        movable = [i for i in range(count - 1) if given[i] < reach]
        whole, budget = sum([loads[i] for i in movable]), rest
        for i in movable:
            extra = min(reach - given[i], max(1, budget * loads[i] // whole), rest)
            given[i] = given[i] + extra
            rest = rest - extra
    return np.array([reach] + given)


def uneven_parts(rng, count, total, reach, skew):
    if count == 2:
        one = jax.random.randint(rng, (), max(1, total - reach), min(reach, total - 1) + 1)
        return jnp.stack([one, total - one])
    sizes = jnp.asarray(profile(count, total, reach, skew), jnp.int32)
    pairs = (count - 1) // 2
    source_of, taker = sizes[1:1 + 2 * pairs:2], sizes[2:2 + 2 * pairs:2]
    room = jnp.minimum(source_of - 1, reach - taker)
    shifted = jax.random.randint(jax.random.fold_in(rng, 1), (pairs,), 0, 1 << 20) % (room + 1)
    sizes = sizes.at[1:1 + 2 * pairs:2].set(source_of - shifted).at[2:2 + 2 * pairs:2].set(taker + shifted)
    return sizes[jax.random.permutation(jax.random.fold_in(rng, 2), count)]


def centred(stream_key, shape, scale, bound, shards=(), held_as=jnp.bfloat16):
    values = scale * jax.random.normal(stream_key, shape, jnp.float32)
    if shards:
        values = values * block_scale(stream_key, shape, shards, -0.22, 0.18)
    return jnp.clip(values, -bound, bound).astype(held_as)


def setup_inputs(seed: int = 0) -> dict:
    arg_keys = jax.random.split(jax.random.key(seed), 8)
    return {
        "queries": draw_queries(jax.random.fold_in(arg_keys[7], 71), 0),
        "keys": draw_keys(jax.random.fold_in(arg_keys[7], 71), 0),
        "values": centred(arg_keys[2], (RELAY_SECTIONS, SEQUENCE_TOKENS, KEY_VALUE_HEADS * HEAD_SIZE), 1.0, 6.0, ((0, 4), (1, 32), (2, 4))),
        "modality": plant(jax.random.randint(arg_keys[3], (RELAY_SECTIONS, SEQUENCE_TOKENS), 0, 2), jax.random.fold_in(arg_keys[3], 1), 0, 1).astype(jnp.int32),
        "query_gain": jnp.clip(1.0 + 0.1 * jax.random.normal(arg_keys[4], (2, QUERY_HEADS * HEAD_SIZE), jnp.float32), 0.5, 1.5),
        "tower_key_gain": jnp.clip(1.0 + 0.1 * jax.random.normal(arg_keys[5], (2, KEY_VALUE_HEADS * HEAD_SIZE), jnp.float32), 0.5, 1.5),
        "doc_lengths": jax.vmap(lambda own: uneven_parts(own, DOCS, SEQUENCE_TOKENS, 5 * SEQUENCE_TOKENS // 8, 2))(jax.random.split(arg_keys[6], RELAY_SECTIONS)).reshape((RELAY_SECTIONS, DOCS)).astype(jnp.int32),
    }


def doc_index(doc_row, places):
    bounds = jnp.cumsum(doc_row)[:-1]
    return jnp.sum((places[:, None] >= bounds[None, :]).astype(jnp.int32), axis=1)


def tower_scaled(inputs, towers, gains):
    chosen = jnp.where(towers[:, None] == 1, gains[1][None, :], gains[0][None, :])
    return (inputs.astype(jnp.float32) * chosen).astype(jnp.bfloat16)


def attend_section(query_row_slice, key_row_slice, value_row_slice, doc_row):
    query_group = QUERY_HEADS // KEY_VALUE_HEADS
    places = jnp.arange(SEQUENCE_TOKENS, dtype=jnp.int32)
    docs = doc_index(doc_row, places)
    complete_keys = key_row_slice.reshape(SEQUENCE_TOKENS, KEY_VALUE_HEADS, HEAD_SIZE).astype(jnp.float32)
    complete_values = value_row_slice.reshape(SEQUENCE_TOKENS, KEY_VALUE_HEADS, HEAD_SIZE).astype(jnp.float32)
    current_block = math.gcd(SEQUENCE_TOKENS, 256)
    block_count = SEQUENCE_TOKENS // current_block
    query_block_list = query_row_slice.reshape(block_count, current_block, KEY_VALUE_HEADS, query_group, HEAD_SIZE)

    def one_block(inputs):
        query_part, index = inputs
        query_places = index * current_block + jnp.arange(current_block, dtype=jnp.int32)
        query_docs = lax.dynamic_slice_in_dim(docs, index * current_block, current_block, 0)
        scores = jnp.einsum("qkgd,tkd->kgqt", query_part.astype(jnp.float32), complete_keys) * HEAD_SIZE ** -0.5
        visible = (places[None, :] <= query_places[:, None]) & (docs[None, :] == query_docs[:, None])
        masked = jnp.where(visible[None, None], scores, -jnp.inf)
        peak = jnp.max(masked, axis=-1, keepdims=True)
        weights = jnp.where(visible[None, None], jnp.exp(scores - peak), 0.0)
        total = jnp.sum(weights, axis=-1)
        rounded = lax.optimization_barrier(weights.astype(jnp.bfloat16)).astype(jnp.float32)
        mixed = jnp.einsum("kgqt,tkd->qkgd", rounded, complete_values)
        mixed = mixed / jnp.transpose(total, (2, 0, 1))[..., None]
        return mixed.reshape(current_block, QUERY_HEADS * HEAD_SIZE).astype(jnp.bfloat16)

    outputs = lax.map(one_block, (query_block_list, jnp.arange(block_count, dtype=jnp.int32)))
    return outputs.reshape(SEQUENCE_TOKENS, QUERY_HEADS * HEAD_SIZE)


def reference(queries, keys, values, modality, query_gain, tower_key_gain, doc_lengths):
    stacked = []
    for section_index in range(RELAY_SECTIONS):
        query_row_slice = tower_scaled(queries[section_index], modality[section_index], query_gain)
        key_row_slice = tower_scaled(keys[section_index], modality[section_index], tower_key_gain)
        stacked.append(attend_section(query_row_slice, key_row_slice, values[section_index], doc_lengths[section_index]))
    attended = jnp.stack(stacked, axis=0)
    return jnp.roll(attended, 1, axis=0)
```

```python
import functools

import jax
import jax.numpy as jnp
from jax import lax
from jax.experimental import pallas as pl
from jax.experimental.pallas import tpu as pltpu
from jax.sharding import PartitionSpec as P

MESH = pl.DeviceIdType.MESH
NT = (((1,), (1,)), ((), ()))
HEAD = 128
ROWS = 192
KV_HEADS = 2
GROUP = 8
HEADS = KV_HEADS * GROUP
BLOCKS = 32
WINDOW = 20
SLOTS = 32
OWN = 31
PER_GROUP = 4
GROUP_KEYS = PER_GROUP * ROWS
KEY_GROUPS = WINDOW // PER_GROUP
BIG = float(1 << 20)
LOG2E = 1.4426950408889634
EXP_SCALE = HEAD ** -0.5 * LOG2E
DIAGONAL = 7

SCHEDULE = (
    (
        0, 64, 129, 193, 258, 322, 387, 451, 516, 580, 612, 645, 677, 709, 774, 838, 870, 903, 935, 1032,
        1096, 1161, 1225, 1290, 1354, 1419, 1483, 1548, 1612, 1677, 1741, 1806, 1870, 1935, 2064, 2128,
        2193, 2257, 2322, 2386, 2451, 2515, 2580, 2644, 2709, 2773, 2838, 2902, 2967, 3160, 3289, 3418,
        3547, 3676, 3805, 3934,
    ),
    (
        128, 192, 257, 321, 386, 450, 484, 515, 579, 646, 678, 708, 773, 837, 902, 1024, 1160, 1224, 1249,
        1289, 1353, 1378, 1418, 1482, 1507, 1540, 1611, 1636, 1669, 1740, 1765, 1798, 1869, 1927, 2023,
        2056, 2192, 2256, 2281, 2314, 2385, 2410, 2443, 2514, 2539, 2572, 2643, 2668, 2708, 2765, 2797,
        2837, 2894, 2926, 2966, 3055, 3288, 3313, 3417, 3442, 3546, 3571, 3675, 3700, 3804, 3829, 3933,
        3958, 4087,
    ),
    (
        256, 320, 356, 385, 449, 514, 578, 643, 707, 772, 836, 901, 1025, 1152, 1250, 1288, 1352, 1379,
        1417, 1481, 1508, 1546, 1610, 1637, 1670, 1707, 1739, 1766, 1804, 1868, 1895, 1933, 2057, 2186,
        2282, 2315, 2384, 2411, 2444, 2513, 2540, 2578, 2642, 2669, 2707, 2771, 2798, 2831, 2901, 2927,
        2958, 3047, 3144, 3280, 3314, 3416, 3443, 3545, 3572, 3674, 3701, 3796, 3830, 3925, 3959, 4071,
    ),
    (
        132, 228, 384, 448, 513, 577, 642, 683, 706, 771, 835, 900, 1026, 1155, 1251, 1280, 1413, 1480,
        1509, 1542, 1609, 1638, 1671, 1738, 1767, 1803, 1867, 1892, 1932, 2058, 2113, 2187, 2283, 2316,
        2376, 2412, 2441, 2512, 2541, 2570, 2641, 2670, 2706, 2770, 2799, 2835, 2899, 2924, 2959, 3145,
        3272, 3315, 3410, 3444, 3544, 3573, 3673, 3702, 3803, 3831, 3892, 3924, 3951, 4078,
    ),
    (
        4, 36, 512, 576, 641, 705, 770, 834, 899, 1027, 1156, 1285, 1381, 1414, 1510, 1543, 1608, 1639,
        1673, 1737, 1802, 1866, 1931, 2059, 2114, 2188, 2243, 2284, 2317, 2368, 2413, 2446, 2504, 2542,
        2576, 2640, 2671, 2705, 2769, 2789, 2834, 2898, 2923, 2956, 3281, 3316, 3408, 3445, 3531, 3574,
        3672, 3703, 3801, 3823, 3932, 3950, 4020,
    ),
    (
        640, 704, 769, 833, 898, 1028, 1157, 1253, 1286, 1382, 1415, 1511, 1538, 1672, 1736, 1801, 1865,
        1925, 2060, 2189, 2242, 2285, 2313, 2371, 2414, 2449, 2496, 2543, 2574, 2628, 2660, 2704, 2768,
        2793, 2828, 2897, 2922, 2955, 3317, 3400, 3446, 3529, 3575, 3627, 3658, 3695, 3800, 3827, 3929,
    ),
    (
        768, 832, 897, 1029, 1158, 1254, 1287, 1383, 1409, 1537, 1667, 1800, 1864, 1930, 2061, 2190, 2244,
        2286, 2310, 2370, 2415, 2439, 2499, 2573, 2626, 2697, 2757, 2829, 2896, 2961, 3318, 3402, 3447,
        3528, 3566, 3660, 3802, 3825, 3922, 4075,
    ),
    (
        896, 1030, 1159, 1255, 1281, 1665, 1794, 1924, 2053, 2182, 2287, 2311, 2445, 2701, 2756, 2832,
        2888, 2960, 3310, 3567, 3793, 3931,
    ),
    (
        1031, 1795, 1923, 2054, 2183, 2826, 2889, 2963, 3141, 3319, 3439, 3930,
    ),
    (
        1926, 2055, 2957, 3311, 3928,
    ),
)
ROUNDS = len(SCHEDULE)


def neighbour(chip, direction):
    x, z = divmod(chip, 8)
    return (
        ((x + 1) % 4) * 8 + z,
        ((x + 3) % 4) * 8 + z,
        chip + 1,
        chip - 1,
    )[direction]


def relay_tables():
    slot = [{chip: OWN} for chip in range(BLOCKS)]
    count = [0] * BLOCKS
    spare = [WINDOW] * BLOCKS
    sends = [[[1023] * ROUNDS for _ in range(4)] for _ in range(BLOCKS)]
    takes = [[[31] * ROUNDS for _ in range(4)] for _ in range(BLOCKS)]
    ready = [[0] * ROUNDS for _ in range(BLOCKS)]
    for step, entries in enumerate(SCHEDULE):
        known = [dict(held) for held in slot]
        for entry in entries:
            link, block = divmod(entry, 32)
            sender, direction = divmod(link, 4)
            target = neighbour(sender, direction)
            if max(0, target - WINDOW) <= block < target:
                place = count[target]
                count[target] += 1
            else:
                place = spare[target]
                spare[target] += 1
            assert place < OWN and block not in slot[target]
            slot[target][block] = place
            sends[sender][direction][step] = known[sender][block] * 32 + place
            takes[target][direction][step] = place
        for chip in range(BLOCKS):
            ready[chip][step] = count[chip] // PER_GROUP
    for chip in range(BLOCKS):
        assert count[chip] == min(chip, WINDOW)
        ready[chip][ROUNDS - 1] = -(-count[chip] // PER_GROUP)
    owners = [[31] * WINDOW for _ in range(BLOCKS)]
    for chip in range(BLOCKS):
        for block, place in slot[chip].items():
            if place < WINDOW:
                owners[chip][place] = block
    return sends, takes, ready, owners, count


def packed(values, bits):
    per = 30 // bits
    return [
        sum(value << (bits * i) for i, value in enumerate(values[at : at + per]))
        for at in range(0, len(values), per)
    ]


def chosen(chip, per_chip):
    result = jnp.int32(per_chip[0])
    for index in range(1, len(per_chip)):
        if per_chip[index] != per_chip[0]:
            result = jnp.where(chip == index, jnp.int32(per_chip[index]), result)
    return result


class Table:
    def __init__(self, chip, per_chip, bits):
        self.bits = bits
        self.per = 30 // bits
        rows = [packed(values, bits) for values in per_chip]
        self.words = [chosen(chip, column) for column in zip(*rows)]

    def at(self, index):
        word = self.words[0]
        for place in range(1, len(self.words)):
            word = jnp.where(index >= place * self.per, self.words[place], word)
        shift = lax.rem(index, self.per) * self.bits
        return lax.shift_right_logical(word, shift) & ((1 << self.bits) - 1)


ITEMS = ((0, 7), (0, 0), (0, 1), (1, 7), (1, 0), (1, 1), (0, 2), (1, 2), (0, 3), (1, 3), (0, 4), (1, 4))
HALVES = 2
UNITS = len(ITEMS) * HALVES
FIRST_STEP = 12
SECOND_STEP = 21
COMM_STEPS = ROUNDS * 4
STEPS = COMM_STEPS + UNITS
QUERY_COPIES = 8


def one_hot_rows(places, first, last):
    inside = (places >= first) & (places < last)
    return inside


def kernel(
    q_ref, k_ref, v_ref, modality_ref, q_gain_ref, k_gain_ref, docs_ref, o_ref,
    kv, key_stage, query_stage, queries, docs_stage, docs_in, key_docs, query_docs,
    peak, total, summed,
    link_send, link_recv, hop_send, hop_recv, query_send, query_recv, docs_sems,
):
    section = lax.axis_index("section")
    chip = lax.axis_index("ctx")
    part = lax.axis_index("tp")
    x, z = chip // 8, lax.rem(chip, 8)
    after = (lax.rem(section + 1, 4), chip, part)
    before = (lax.rem(section + 3, 4), chip, part)
    around = (
        (section, lax.rem(x + 1, 4) * 8 + z, part),
        (section, lax.rem(x + 3, 4) * 8 + z, part),
        (section, x * 8 + jnp.minimum(z + 1, 7), part),
        (section, x * 8 + jnp.maximum(z - 1, 0), part),
    )
    exists = (None, None, z < 7, z > 0)

    barrier = pltpu.get_barrier_semaphore()
    for device in (after, before, around[0], around[1]):
        pl.semaphore_signal(barrier, inc=1, device_id=device, device_id_type=MESH)
    for direction in (2, 3):
        @pl.when(exists[direction])
        def _():
            pl.semaphore_signal(barrier, inc=1, device_id=around[direction], device_id_type=MESH)
    pl.semaphore_wait(barrier, 4 + (z < 7).astype(jnp.int32) + (z > 0).astype(jnp.int32))

    diagonal = lax.broadcasted_iota(jnp.int32, (ROWS, ROWS), 0) == lax.broadcasted_iota(
        jnp.int32, (ROWS, ROWS), 1
    )
    towers = jnp.sum(
        jnp.where(diagonal, modality_ref[0:1, :].astype(jnp.float32), 0.0), axis=1, keepdims=True
    )
    image = jnp.broadcast_to(towers, (ROWS, HEAD)) > 0.5

    def scaled(values, gain_ref, channels):
        gains = jnp.where(image, gain_ref[1:2, channels], gain_ref[0:1, channels])
        return (values.astype(jnp.float32) * gains).astype(jnp.bfloat16)

    def hop(stream):
        head, kind = stream // 2, stream % 2
        if kind == 0:
            source = key_stage.at[head]
        else:
            source = v_ref.at[0, :, pl.ds(head * HEAD, HEAD)]
        return pltpu.make_async_remote_copy(
            src_ref=source, dst_ref=kv.at[head, OWN, kind],
            send_sem=hop_send.at[stream], recv_sem=hop_recv.at[stream],
            device_id=after, device_id_type=MESH,
        )

    for head in range(KV_HEADS):
        channels = pl.ds(head * HEAD, HEAD)
        key_stage[head] = scaled(k_ref[0, :, channels], k_gain_ref, channels)
        hop(2 * head).start()
        hop(2 * head + 1).start()

    docs_stage[...] = jnp.zeros_like(docs_stage)
    docs_stage[0:1, 0:16] = docs_ref[...]
    docs_copy = pltpu.make_async_remote_copy(
        src_ref=docs_stage, dst_ref=docs_in, send_sem=docs_sems.at[0], recv_sem=docs_sems.at[1],
        device_id=after, device_id_type=MESH,
    )
    docs_copy.start()

    sends, takes, ready, owners, count = relay_tables()
    send_tables = [Table(chip, [sends[c][d] for c in range(BLOCKS)], 10) for d in range(4)]
    take_tables = [Table(chip, [takes[c][d] for c in range(BLOCKS)], 5) for d in range(4)]
    ready_table = Table(chip, ready, 3)
    owner_table = Table(chip, owners, 5)
    arrivals = jnp.minimum(chip, WINDOW)
    groups = (arrivals + PER_GROUP - 1) // PER_GROUP

    def link_copy(direction, step, stream, source, target):
        head, kind = stream // 2, lax.rem(stream, 2)
        return pltpu.make_async_remote_copy(
            src_ref=kv.at[head, source, kind], dst_ref=kv.at[head, target, kind],
            send_sem=link_send.at[direction, step, stream],
            recv_sem=link_recv.at[direction, step, stream],
            device_id=around[direction], device_id_type=MESH,
        )

    def start_round(step, stream):
        for direction in range(4):
            code = send_tables[direction].at(step)

            @pl.when(code != 1023)
            def _():
                link_copy(direction, step, stream, code // 32, lax.rem(code, 32)).start()

    def take_round(step, stream):
        for direction in range(4):
            place = take_tables[direction].at(step)

            @pl.when(place != 31)
            def _():
                link_copy(direction, step, stream, place, place).wait_recv()

    def query_copy(index):
        heads = pl.ds(index * (HEADS // QUERY_COPIES), HEADS // QUERY_COPIES)
        return pltpu.make_async_remote_copy(
            src_ref=query_stage.at[heads], dst_ref=queries.at[heads],
            send_sem=query_send.at[index], recv_sem=query_recv.at[index],
            device_id=after, device_id_type=MESH,
        )

    for head in range(HEADS):
        channels = pl.ds(head * HEAD, HEAD)
        query_stage[head] = scaled(q_ref[0, :, channels], q_gain_ref, channels)

    for stream in range(4):
        hop(stream).wait_recv()
        start_round(jnp.int32(0), jnp.int32(stream))
    for index in range(QUERY_COPIES):
        query_copy(index).start()

    def clear(place, carry):
        for head in range(KV_HEADS):
            kv[head, place] = jnp.zeros((2, ROWS, HEAD), jnp.bfloat16)
        return carry

    lax.fori_loop(arrivals, groups * PER_GROUP, clear, 0)

    docs_copy.wait_recv()
    lengths = docs_in[0:1, :].astype(jnp.float32)
    square = (HEAD, HEAD)
    down = lax.broadcasted_iota(jnp.int32, square, 0)
    across = lax.broadcasted_iota(jnp.int32, square, 1)
    column = jnp.sum(jnp.where(down == across, lengths, 0.0), axis=1, keepdims=True)
    first = jnp.sum(jnp.where(down < across, column, 0.0), axis=0, keepdims=True)
    lane = lax.broadcasted_iota(jnp.int32, (1, HEAD), 1)
    last = jnp.where(lane == 15, 1e9, first + lengths)
    first = jnp.where(lane < 16, first, jnp.where(lane == 16, -1e9, 1e9))
    last = jnp.where(lane < 16, last, jnp.where(lane == 16, 0.0, 1e9))
    inner = lax.broadcasted_iota(jnp.int32, (ROWS, HEAD), 0)

    def members(block):
        places = (inner + block * ROWS).astype(jnp.float32)
        return (places >= first) & (places < last)

    def mark(place, carry):
        block = jnp.where(place < arrivals, owner_table.at(place), -1)
        key_docs[place] = jnp.where(members(block), 1.0, 0.0).astype(jnp.bfloat16)
        return carry

    lax.fori_loop(0, groups * PER_GROUP, mark, 0)
    own_members = members(chip)
    key_docs[WINDOW] = jnp.where(own_members, 1.0, 0.0).astype(jnp.bfloat16)
    query_docs[...] = jnp.where(own_members, 0.0, -BIG).astype(jnp.bfloat16)

    heads_per_unit = GROUP // HALVES
    causal = lax.broadcasted_iota(jnp.int32, (ROWS, ROWS), 1) <= lax.broadcasted_iota(
        jnp.int32, (ROWS, ROWS), 0
    )

    def attend_own(head, half):
        keys = jnp.concatenate([kv[head, OWN, 0], key_docs[WINDOW]], axis=1)
        values = jnp.concatenate([kv[head, OWN, 1], jnp.ones((ROWS, HEAD), jnp.bfloat16)], axis=1)
        marks = query_docs[...]
        for index in range(heads_per_unit):
            row = head * GROUP + half * heads_per_unit + index
            rows = jnp.concatenate([queries[row], marks], axis=1)
            scores = lax.dot_general(rows, keys, NT, preferred_element_type=jnp.float32)
            scores = jnp.where(causal, scores, -1e30)
            top = jnp.max(scores, axis=1, keepdims=True)
            weights = jnp.exp2((scores - top) * EXP_SCALE).astype(jnp.bfloat16)
            mixed = jnp.dot(weights, values, preferred_element_type=jnp.float32)
            peak[row] = jnp.broadcast_to(top, (ROWS, HEAD))
            summed[row] = mixed[:, :HEAD]
            total[row] = mixed[:, HEAD:]

    def attend_group(head, group, half):
        slots = pl.ds(group * PER_GROUP, PER_GROUP)
        keys = jnp.concatenate(
            [kv[head, slots, 0].reshape(GROUP_KEYS, HEAD), key_docs[slots].reshape(GROUP_KEYS, HEAD)],
            axis=1,
        )
        values = jnp.concatenate(
            [kv[head, slots, 1].reshape(GROUP_KEYS, HEAD), jnp.ones((GROUP_KEYS, HEAD), jnp.bfloat16)],
            axis=1,
        )
        marks = query_docs[...]
        for index in range(heads_per_unit):
            row = head * GROUP + half * heads_per_unit + index
            rows = jnp.concatenate([queries[row], marks], axis=1)
            scores = lax.dot_general(rows, keys, NT, preferred_element_type=jnp.float32)
            old = peak[row]
            new = jnp.maximum(old, jnp.max(scores, axis=1, keepdims=True))
            shrink = jnp.exp2((old - new) * EXP_SCALE)
            weights = jnp.exp2((scores - new[:, 0:1]) * EXP_SCALE).astype(jnp.bfloat16)
            mixed = jnp.dot(weights, values, preferred_element_type=jnp.float32)
            peak[row] = new
            summed[row] = summed[row] * shrink + mixed[:, :HEAD]
            total[row] = total[row] * shrink + mixed[:, HEAD:]

    item_words = packed([head * 8 + group for head, group in ITEMS], 4)

    def step_body(index, done):
        step, stream = index // 4, lax.rem(index, 4)
        at = jnp.minimum(step, ROUNDS - 1)

        @pl.when(step < ROUNDS)
        def _():
            take_round(step, stream)

            @pl.when(step + 1 < ROUNDS)
            def _():
                start_round(step + 1, stream)

        @pl.when(index == FIRST_STEP)
        def _():
            for copy in range(QUERY_COPIES // 2):
                query_copy(copy).wait_recv()

        @pl.when(index == SECOND_STEP)
        def _():
            for copy in range(QUERY_COPIES // 2, QUERY_COPIES):
                query_copy(copy).wait_recv()

        unit = jnp.minimum(done, UNITS - 1)
        item, half = unit // HALVES, lax.rem(unit, HALVES)
        word = jnp.where(item >= 7, jnp.int32(item_words[1]), jnp.int32(item_words[0]))
        code = lax.shift_right_logical(word, lax.rem(item, 7) * 4) & 15
        head, group = code // 8, lax.rem(code, 8)
        now = ready_table.at(at)
        past = jnp.where(step == 0, 0, ready_table.at(jnp.maximum(at - 1, 0)))
        arrived = jnp.where(
            step >= ROUNDS, groups, jnp.where(stream >= jnp.where(head == 0, 1, 3), now, past)
        )
        empty = (group != DIAGONAL) & (group >= groups)
        open_now = (group == DIAGONAL) | (group < arrived) | empty
        open_now = open_now & (index >= jnp.where(head == 0, FIRST_STEP, SECOND_STEP))
        open_now = open_now & (done < UNITS)

        @pl.when(open_now & (group == DIAGONAL))
        def _():
            attend_own(head, half)

        @pl.when(open_now & (group != DIAGONAL) & (group < groups))
        def _():
            attend_group(head, group, half)

        return done + open_now.astype(jnp.int32)

    lax.fori_loop(0, STEPS, step_body, jnp.int32(0))

    for head in range(HEADS):
        o_ref[0, :, pl.ds(head * HEAD, HEAD)] = (summed[head] / total[head]).astype(jnp.bfloat16)

    def drain(step, carry):
        for direction in range(4):
            code = send_tables[direction].at(step)

            @pl.when(code != 1023)
            def _():
                for stream in range(4):
                    link_copy(direction, step, stream, code // 32, lax.rem(code, 32)).wait_send()
        return carry

    lax.fori_loop(0, ROUNDS, drain, 0)
    for stream in range(4):
        hop(stream).wait_send()
    for index in range(QUERY_COPIES):
        query_copy(index).wait_send()
    docs_copy.wait_send()


def body(queries, keys, values, modality, query_gain, tower_key_gain, doc_lengths):
    vmem = pl.BlockSpec(memory_space=pltpu.VMEM)
    dma = pltpu.SemaphoreType.DMA
    return pl.pallas_call(
        kernel,
        out_shape=jax.ShapeDtypeStruct(queries.shape, jnp.bfloat16),
        in_specs=[vmem] * 7,
        out_specs=vmem,
        scratch_shapes=[
            pltpu.VMEM((KV_HEADS, SLOTS, 2, ROWS, HEAD), jnp.bfloat16),
            pltpu.VMEM((KV_HEADS, ROWS, HEAD), jnp.bfloat16),
            pltpu.VMEM((HEADS, ROWS, HEAD), jnp.bfloat16),
            pltpu.VMEM((HEADS, ROWS, HEAD), jnp.bfloat16),
            pltpu.VMEM((8, HEAD), jnp.int32),
            pltpu.VMEM((8, HEAD), jnp.int32),
            pltpu.VMEM((WINDOW + 1, ROWS, HEAD), jnp.bfloat16),
            pltpu.VMEM((ROWS, HEAD), jnp.bfloat16),
            pltpu.VMEM((HEADS, ROWS, HEAD), jnp.float32),
            pltpu.VMEM((HEADS, ROWS, HEAD), jnp.float32),
            pltpu.VMEM((HEADS, ROWS, HEAD), jnp.float32),
            dma((4, ROUNDS, 4)),
            dma((4, ROUNDS, 4)),
            dma((4,)),
            dma((4,)),
            dma((QUERY_COPIES,)),
            dma((QUERY_COPIES,)),
            dma((2,)),
        ],
        compiler_params=pltpu.CompilerParams(
            collective_id=3, has_side_effects=True, vmem_limit_bytes=48 * 2**20
        ),
        name="relayed_attention",
    )(queries, keys, values, modality, query_gain, tower_key_gain, doc_lengths)


def solution(mesh):
    placed = (
        P("section", "ctx", "tp"),
        P("section", "ctx", "tp"),
        P("section", "ctx", "tp"),
        P("section", "ctx"),
        P(None, "tp"),
        P(None, "tp"),
        P("section", None),
    )
    return jax.shard_map(
        body, mesh=mesh, in_specs=placed, out_specs=P("section", "ctx", "tp"), check_vma=False
    )
```

```python
import functools

import jax
import jax.numpy as jnp
from jax import lax
from jax.experimental import pallas as pl
from jax.experimental.pallas import tpu as pltpu
from jax.sharding import PartitionSpec as P

MESH = pl.DeviceIdType.MESH
NT = (((1,), (1,)), ((), ()))
HEAD = 128
ROWS = 192
KV_HEADS = 2
GROUP = 8
HEADS = KV_HEADS * GROUP
BLOCKS = 32
WINDOW = 20
SLOTS = 32
OWN = 31
PER_GROUP = 4
GROUP_KEYS = PER_GROUP * ROWS
KEY_GROUPS = WINDOW // PER_GROUP
BIG = float(1 << 20)
LOG2E = 1.4426950408889634
EXP_SCALE = HEAD ** -0.5 * LOG2E
DIAGONAL = 7

SCHEDULE = (
    (
        0, 64, 129, 193, 258, 290, 322, 387, 419, 451, 516, 548, 580, 612, 645, 677, 709, 741, 774, 806,
        838, 870, 903, 935, 999, 1032, 1096, 1161, 1225, 1290, 1322, 1354, 1419, 1451, 1483, 1548, 1580,
        1612, 1677, 1709, 1741, 1806, 1870, 1935, 1967, 2064, 2128, 2193, 2257, 2322, 2386, 2451, 2515,
        2580, 2644, 2709, 2773, 2838, 2902, 2967, 3160, 3289, 3418, 3547, 3676, 3805, 3934,
    ),
    (
        192, 289, 321, 386, 427, 450, 484, 515, 549, 579, 613, 644, 685, 708, 742, 773, 805, 837, 871, 902,
        943, 1024, 1153, 1224, 1249, 1289, 1321, 1353, 1378, 1418, 1450, 1482, 1507, 1547, 1579, 1611,
        1636, 1676, 1708, 1740, 1765, 1805, 1869, 1894, 1934, 1966, 2023, 2056, 2120, 2185, 2256, 2281,
        2321, 2385, 2410, 2450, 2514, 2539, 2579, 2643, 2668, 2708, 2772, 2797, 2830, 2901, 2926, 2966,
        3055, 3152, 3288, 3313, 3362, 3417, 3442, 3546, 3571, 3620, 3675, 3700, 3749, 3804, 3829, 3878,
        3933, 3958, 4007, 4087,
    ),
    (
        128, 256, 297, 320, 356, 385, 426, 449, 485, 514, 555, 578, 614, 643, 684, 707, 743, 772, 804, 836,
        901, 942, 1025, 1154, 1217, 1250, 1283, 1352, 1379, 1410, 1449, 1481, 1508, 1539, 1578, 1610, 1637,
        1668, 1707, 1739, 1766, 1804, 1868, 1895, 1926, 1965, 2057, 2112, 2186, 2248, 2282, 2315, 2384,
        2411, 2444, 2513, 2540, 2578, 2642, 2669, 2707, 2771, 2798, 2829, 2900, 2927, 2965, 3047, 3144,
        3280, 3314, 3361, 3416, 3443, 3491, 3545, 3572, 3621, 3674, 3701, 3803, 3830, 3877, 3932, 3959,
        4079,
    ),
    (
        132, 228, 298, 357, 390, 425, 448, 486, 513, 554, 577, 615, 642, 683, 706, 771, 803, 835, 900, 941,
        1026, 1155, 1251, 1284, 1344, 1413, 1480, 1509, 1545, 1609, 1667, 1706, 1738, 1767, 1803, 1835,
        1867, 1925, 1964, 2058, 2187, 2240, 2283, 2316, 2376, 2412, 2449, 2512, 2541, 2574, 2641, 2670,
        2706, 2770, 2799, 2828, 2899, 2918, 2964, 3272, 3315, 3408, 3444, 3544, 3573, 3673, 3702, 3802,
        3831, 3876, 3931, 3951, 4085,
    ),
    (
        36, 165, 229, 294, 358, 391, 423, 487, 556, 576, 641, 674, 705, 770, 811, 834, 899, 940, 1027,
        1156, 1252, 1285, 1381, 1408, 1472, 1510, 1537, 1608, 1673, 1737, 1802, 1834, 1866, 1924, 1963,
        2059, 2188, 2284, 2317, 2369, 2413, 2446, 2504, 2542, 2569, 2640, 2671, 2705, 2769, 2790, 2834,
        2898, 2919, 2963, 3316, 3400, 3445, 3497, 3536, 3574, 3626, 3672, 3703, 3755, 3801, 3823, 3875,
        3930, 3950, 4013, 4084,
    ),
    (
        37, 166, 230, 295, 359, 640, 682, 704, 769, 810, 833, 898, 939, 1253, 1286, 1382, 1414, 1511, 1538,
        1665, 1736, 1794, 1865, 1930, 2060, 2189, 2285, 2318, 2372, 2414, 2445, 2496, 2543, 2573, 2632,
        2697, 2768, 2791, 2833, 2897, 2922, 2962, 3108, 3237, 3317, 3446, 3495, 3528, 3575, 3664, 3695,
        3746, 3800, 3825, 3929, 4012, 4083,
    ),
    (
        38, 167, 231, 832, 897, 1158, 1254, 1287, 1383, 1728, 1801, 1864, 1929, 2061, 2190, 2286, 2415,
        2760, 2896, 2961, 3109, 3318, 3447, 3567, 3792, 3928, 4011,
    ),
    (
        39, 1030, 1255, 1856, 1923, 2062, 2191, 2287, 2888, 3239, 3319, 3920,
    ),
    (
        2063, 3111,
    ),
)
ROUNDS = len(SCHEDULE)


def neighbour(chip, direction):
    x, z = divmod(chip, 8)
    return (
        ((x + 1) % 4) * 8 + z,
        ((x + 3) % 4) * 8 + z,
        chip + 1,
        chip - 1,
    )[direction]


def relay_tables():
    slot = [{chip: OWN} for chip in range(BLOCKS)]
    count = [0] * BLOCKS
    spare = [WINDOW] * BLOCKS
    sends = [[[1023] * ROUNDS for _ in range(4)] for _ in range(BLOCKS)]
    takes = [[[31] * ROUNDS for _ in range(4)] for _ in range(BLOCKS)]
    ready = [[0] * ROUNDS for _ in range(BLOCKS)]
    for step, entries in enumerate(SCHEDULE):
        known = [dict(held) for held in slot]
        for entry in entries:
            link, block = divmod(entry, 32)
            sender, direction = divmod(link, 4)
            target = neighbour(sender, direction)
            if max(0, target - WINDOW) <= block < target:
                place = count[target]
                count[target] += 1
            else:
                place = spare[target]
                spare[target] += 1
            assert place < OWN and block not in slot[target]
            slot[target][block] = place
            sends[sender][direction][step] = known[sender][block] * 32 + place
            takes[target][direction][step] = place
        for chip in range(BLOCKS):
            ready[chip][step] = count[chip] // PER_GROUP
    for chip in range(BLOCKS):
        assert count[chip] == min(chip, WINDOW)
        ready[chip][ROUNDS - 1] = -(-count[chip] // PER_GROUP)
    owners = [[31] * WINDOW for _ in range(BLOCKS)]
    for chip in range(BLOCKS):
        for block, place in slot[chip].items():
            if place < WINDOW:
                owners[chip][place] = block
    return sends, takes, ready, owners, count


def packed(values, bits):
    per = 30 // bits
    return [
        sum(value << (bits * i) for i, value in enumerate(values[at : at + per]))
        for at in range(0, len(values), per)
    ]


def chosen(chip, per_chip):
    result = jnp.int32(per_chip[0])
    for index in range(1, len(per_chip)):
        if per_chip[index] != per_chip[0]:
            result = jnp.where(chip == index, jnp.int32(per_chip[index]), result)
    return result


class Table:
    def __init__(self, chip, per_chip, bits):
        self.bits = bits
        self.per = 30 // bits
        rows = [packed(values, bits) for values in per_chip]
        self.words = [chosen(chip, column) for column in zip(*rows)]

    def at(self, index):
        word = self.words[0]
        for place in range(1, len(self.words)):
            word = jnp.where(index >= place * self.per, self.words[place], word)
        shift = lax.rem(index, self.per) * self.bits
        return lax.shift_right_logical(word, shift) & ((1 << self.bits) - 1)


TILE_HEADS = 4
TILE_ROWS = TILE_HEADS * ROWS
TILES = GROUP // TILE_HEADS
STREAMS = 2 * KV_HEADS
FIRST_STEP = 5
SECOND_STEP = 9
CHUNKS = ROUNDS * KV_HEADS + KV_HEADS * (KEY_GROUPS + 1)
QUERY_COPIES = 8


def kernel(
    q_hbm, k_hbm, v_hbm, modality_hbm, q_gain_hbm, k_gain_hbm, docs_hbm, o_ref,
    q_in, k_in, modality, q_gain, k_gain, docs_own,
    kv, key_stage, query_stage, queries, docs_stage, docs_in, key_docs, query_docs,
    peak, total, summed,
    load_sems, link_send, link_recv, hop_send, hop_recv, query_send, query_recv, docs_sems,
):
    loads = [
        pltpu.make_async_copy(source, target, load_sems.at[index])
        for index, (source, target) in enumerate(
            (
                (k_hbm, k_in), (modality_hbm, modality), (k_gain_hbm, k_gain), (docs_hbm, docs_own),
                (q_gain_hbm, q_gain), (q_hbm, q_in),
            )
        )
    ]
    for load in loads:
        load.start()

    section = lax.axis_index("section")
    chip = lax.axis_index("ctx")
    part = lax.axis_index("tp")
    x, z = chip // 8, lax.rem(chip, 8)
    after = (lax.rem(section + 1, 4), chip, part)
    before = (lax.rem(section + 3, 4), chip, part)
    around = (
        (section, lax.rem(x + 1, 4) * 8 + z, part),
        (section, lax.rem(x + 3, 4) * 8 + z, part),
        (section, x * 8 + jnp.minimum(z + 1, 7), part),
        (section, x * 8 + jnp.maximum(z - 1, 0), part),
    )
    exists = (None, None, z < 7, z > 0)

    barrier = pltpu.get_barrier_semaphore()
    for device in (after, before, around[0], around[1]):
        pl.semaphore_signal(barrier, inc=1, device_id=device, device_id_type=MESH)
    for direction in (2, 3):
        @pl.when(exists[direction])
        def _():
            pl.semaphore_signal(barrier, inc=1, device_id=around[direction], device_id_type=MESH)

    for load in loads[:3]:
        load.wait()
    diagonal = lax.broadcasted_iota(jnp.int32, (ROWS, ROWS), 0) == lax.broadcasted_iota(
        jnp.int32, (ROWS, ROWS), 1
    )
    towers = jnp.sum(
        jnp.where(diagonal, modality[0:1, :].astype(jnp.float32), 0.0), axis=1, keepdims=True
    )
    image = jnp.broadcast_to(towers, (ROWS, HEAD)) > 0.5

    def scaled(values, gain_ref, channels):
        gains = jnp.where(image, gain_ref[1:2, channels], gain_ref[0:1, channels])
        return (values.astype(jnp.float32) * gains).astype(jnp.bfloat16)

    for head in range(KV_HEADS):
        channels = pl.ds(head * HEAD, HEAD)
        key_stage[head] = scaled(k_in[0, :, channels], k_gain, channels)

    pl.semaphore_wait(barrier, 4 + (z < 7).astype(jnp.int32) + (z > 0).astype(jnp.int32))

    def hop(head, kind):
        if kind == 0:
            source = key_stage.at[head]
        else:
            source = v_hbm.at[0, :, pl.ds(head * HEAD, HEAD)]
        return pltpu.make_async_remote_copy(
            src_ref=source, dst_ref=kv.at[head, OWN, kind],
            send_sem=hop_send.at[head, kind], recv_sem=hop_recv.at[head, kind],
            device_id=after, device_id_type=MESH,
        )

    for head in range(KV_HEADS):
        for kind in range(2):
            hop(head, kind).start()

    loads[3].wait()
    docs_stage[...] = jnp.zeros_like(docs_stage)
    docs_stage[0:1, 0:16] = docs_own[...]
    docs_copy = pltpu.make_async_remote_copy(
        src_ref=docs_stage, dst_ref=docs_in, send_sem=docs_sems.at[0], recv_sem=docs_sems.at[1],
        device_id=after, device_id_type=MESH,
    )
    docs_copy.start()

    sends, takes, ready, owners, count = relay_tables()
    send_tables = [Table(chip, [sends[c][d] for c in range(BLOCKS)], 10) for d in range(4)]
    take_tables = [Table(chip, [takes[c][d] for c in range(BLOCKS)], 5) for d in range(4)]
    ready_table = Table(chip, ready, 3)
    owner_table = Table(chip, owners, 5)
    arrivals = jnp.minimum(chip, WINDOW)
    groups = (arrivals + PER_GROUP - 1) // PER_GROUP

    def link_copy(direction, step, head, kind, source, target):
        return pltpu.make_async_remote_copy(
            src_ref=kv.at[head, source, kind], dst_ref=kv.at[head, target, kind],
            send_sem=link_send.at[direction, step, 2 * head + kind],
            recv_sem=link_recv.at[direction, step, 2 * head + kind],
            device_id=around[direction], device_id_type=MESH,
        )

    def start_round(codes, step, head, kind):
        for direction in range(4):
            code = codes[direction]

            @pl.when(code != 1023)
            def _():
                link_copy(direction, step, head, kind, code // 32, lax.rem(code, 32)).start()

    def take_round(places, step, head, kind):
        for direction in range(4):
            place = places[direction]

            @pl.when(place != 31)
            def _():
                link_copy(direction, step, head, kind, place, place).wait_recv()

    def query_copy(index):
        heads = pl.ds(index * (HEADS // QUERY_COPIES), HEADS // QUERY_COPIES)
        return pltpu.make_async_remote_copy(
            src_ref=query_stage.at[heads], dst_ref=queries.at[heads],
            send_sem=query_send.at[index], recv_sem=query_recv.at[index],
            device_id=after, device_id_type=MESH,
        )

    loads[4].wait()
    loads[5].wait()

    def scale_queries(kv_head):
        for head in range(kv_head * GROUP, (kv_head + 1) * GROUP):
            channels = pl.ds(head * HEAD, HEAD)
            query_stage[head] = scaled(q_in[0, :, channels], q_gain, channels)

    scale_queries(0)
    for index in range(QUERY_COPIES // 2):
        query_copy(index).start()
    first_codes = [table.at(0) for table in send_tables]
    for head in range(KV_HEADS):
        for kind in range(2):
            hop(head, kind).wait_recv()
            start_round(first_codes, 0, head, kind)
    scale_queries(1)
    for index in range(QUERY_COPIES // 2, QUERY_COPIES):
        query_copy(index).start()

    def clear(place, carry):
        for head in range(KV_HEADS):
            kv[head, place] = jnp.zeros((2, ROWS, HEAD), jnp.bfloat16)
        return carry

    lax.fori_loop(arrivals, groups * PER_GROUP, clear, 0)

    docs_copy.wait_recv()
    lengths = docs_in[0:1, :].astype(jnp.float32)
    square = (HEAD, HEAD)
    down = lax.broadcasted_iota(jnp.int32, square, 0)
    across = lax.broadcasted_iota(jnp.int32, square, 1)
    column = jnp.sum(jnp.where(down == across, lengths, 0.0), axis=1, keepdims=True)
    first = jnp.sum(jnp.where(down < across, column, 0.0), axis=0, keepdims=True)
    lane = lax.broadcasted_iota(jnp.int32, (1, HEAD), 1)
    last = jnp.where(lane == 15, 1e9, first + lengths)
    first = jnp.where(lane < 16, first, jnp.where(lane == 16, -1e9, 1e9))
    last = jnp.where(lane < 16, last, jnp.where(lane == 16, 0.0, 1e9))
    inner = lax.broadcasted_iota(jnp.int32, (ROWS, HEAD), 0)

    def members(block):
        places = (inner + block * ROWS).astype(jnp.float32)
        return (places >= first) & (places < last)

    def mark(place, carry):
        block = jnp.where(place < arrivals, owner_table.at(place), -1)
        key_docs[place] = jnp.where(members(block), 1.0, 0.0).astype(jnp.bfloat16)
        return carry

    lax.fori_loop(0, groups * PER_GROUP, mark, 0)
    own_members = members(chip)
    key_docs[WINDOW] = jnp.where(own_members, 1.0, 0.0).astype(jnp.bfloat16)
    query_docs[...] = jnp.where(own_members, 0.0, -BIG).astype(jnp.bfloat16)

    def tiles_of(head, keys, values, size, fresh):
        keys, marked = keys
        keys = jnp.concatenate([keys.reshape(size, HEAD), marked.reshape(size, HEAD)], axis=1)
        values = jnp.concatenate(
            [values.reshape(size, HEAD), jnp.ones((size, HEAD), jnp.bfloat16)], axis=1
        )
        marks = jnp.concatenate([query_docs[...]] * TILE_HEADS, axis=0)
        shape = (TILE_HEADS, ROWS, HEAD)

        def rows_of(tile):
            return pl.ds(head * GROUP + tile * TILE_HEADS, TILE_HEADS)

        def score(tile):
            rows = queries[rows_of(tile)].reshape(TILE_ROWS, HEAD)
            rows = jnp.concatenate([rows, marks], axis=1)
            return lax.dot_general(rows, keys, NT, preferred_element_type=jnp.float32)

        scores = {0: score(0)}
        held = {}
        for tile in range(TILES + 1):
            if tile + 1 < TILES:
                scores[tile + 1] = score(tile + 1)
            if tile >= 1:
                weights, shrink = held.pop(tile - 1)
                rows = rows_of(tile - 1)
                mixed = jnp.dot(weights, values, preferred_element_type=jnp.float32)
                if fresh:
                    summed[rows] = mixed[:, :HEAD].reshape(shape)
                    total[rows] = mixed[:, HEAD:].reshape(shape)
                else:
                    summed[rows] = summed[rows] * shrink + mixed[:, :HEAD].reshape(shape)
                    total[rows] = total[rows] * shrink + mixed[:, HEAD:].reshape(shape)
            if tile < TILES:
                rows = rows_of(tile)
                now = scores.pop(tile)
                if fresh:
                    below = lax.broadcasted_iota(jnp.int32, shape[:1] + (ROWS, ROWS), 1)
                    below = below >= lax.broadcasted_iota(jnp.int32, shape[:1] + (ROWS, ROWS), 2)
                    now = jnp.where(below, now.reshape(shape[:1] + (ROWS, ROWS)), -1e30)
                    now = now.reshape(TILE_ROWS, ROWS)
                    new = jnp.broadcast_to(
                        jnp.max(now, axis=1, keepdims=True), (TILE_ROWS, HEAD)
                    )
                    shrink = None
                else:
                    old = peak[rows].reshape(TILE_ROWS, HEAD)
                    new = jnp.maximum(old, jnp.max(now, axis=1, keepdims=True))
                    shrink = jnp.exp2((old - new) * EXP_SCALE).reshape(shape)
                weights = jnp.exp2((now - new[:, 0:1]) * EXP_SCALE).astype(jnp.bfloat16)
                peak[rows] = new.reshape(shape)
                held[tile] = (weights, shrink)

    def step_body(index, done):
        step, stream = index // KV_HEADS, lax.rem(index, KV_HEADS)
        at = jnp.minimum(step, ROUNDS - 1)
        later = jnp.minimum(step + 1, ROUNDS - 1)

        @pl.when(step < ROUNDS)
        def _():
            places = [table.at(at) for table in take_tables]
            codes = [
                jnp.where(step + 1 < ROUNDS, table.at(later), 1023) for table in send_tables
            ]
            for kind in range(2):
                take_round(places, at, stream, kind)
                start_round(codes, later, stream, kind)

        @pl.when(index == FIRST_STEP)
        def _():
            for copy in range(QUERY_COPIES // 2):
                query_copy(copy).wait_recv()

        @pl.when(index == SECOND_STEP)
        def _():
            for copy in range(QUERY_COPIES // 2, QUERY_COPIES):
                query_copy(copy).wait_recv()

        now = jnp.where(step >= ROUNDS, groups, ready_table.at(at))
        past = jnp.where(step == 0, 0, ready_table.at(jnp.maximum(at - 1, 0)))
        past = jnp.where(step >= ROUNDS, groups, past)
        open_first = jnp.where(index >= FIRST_STEP, 1 + now, 0) - done[0]
        open_second = jnp.where(
            index >= SECOND_STEP, 1 + jnp.where(stream == 1, now, past), 0
        ) - done[1]
        pick_first = (open_first > 0) & ((done[0] <= done[1]) | (open_second <= 0))
        pick_second = (open_second > 0) & jnp.logical_not(pick_first)
        head = pick_second.astype(jnp.int32)
        place = jnp.where(pick_second, done[1], done[0])
        some = pick_first | pick_second

        @pl.when(some & (place == 0))
        def _():
            tiles_of(head, (kv[head, OWN, 0], key_docs[WINDOW]), kv[head, OWN, 1], ROWS, True)

        @pl.when(some & (place > 0))
        def _():
            slots = pl.ds((place - 1) * PER_GROUP, PER_GROUP)
            tiles_of(
                head, (kv[head, slots, 0], key_docs[slots]), kv[head, slots, 1], GROUP_KEYS, False
            )

        return (done[0] + pick_first.astype(jnp.int32), done[1] + pick_second.astype(jnp.int32))

    lax.fori_loop(0, CHUNKS, step_body, (jnp.int32(0), jnp.int32(0)))

    for head in range(HEADS):
        o_ref[0, :, pl.ds(head * HEAD, HEAD)] = (summed[head] / total[head]).astype(jnp.bfloat16)

    def drain(step, carry):
        for direction in range(4):
            code = send_tables[direction].at(step)

            @pl.when(code != 1023)
            def _():
                for head in range(KV_HEADS):
                    for kind in range(2):
                        link_copy(
                            direction, step, head, kind, code // 32, lax.rem(code, 32)
                        ).wait_send()
        return carry

    lax.fori_loop(0, ROUNDS, drain, 0)
    for head in range(KV_HEADS):
        hop(head, 0).wait_send()
        hop(head, 1).wait_send()
    for index in range(QUERY_COPIES):
        query_copy(index).wait_send()
    docs_copy.wait_send()


def body(queries, keys, values, modality, query_gain, tower_key_gain, doc_lengths):
    vmem = pl.BlockSpec(memory_space=pltpu.VMEM)
    dma = pltpu.SemaphoreType.DMA
    return pl.pallas_call(
        kernel,
        out_shape=jax.ShapeDtypeStruct(queries.shape, jnp.bfloat16),
        in_specs=[pl.BlockSpec(memory_space=pltpu.HBM)] * 7,
        out_specs=vmem,
        scratch_shapes=[
            pltpu.VMEM(queries.shape, jnp.bfloat16),
            pltpu.VMEM(keys.shape, jnp.bfloat16),
            pltpu.VMEM(modality.shape, jnp.int32),
            pltpu.VMEM(query_gain.shape, jnp.float32),
            pltpu.VMEM(tower_key_gain.shape, jnp.float32),
            pltpu.VMEM(doc_lengths.shape, jnp.int32),
            pltpu.VMEM((KV_HEADS, SLOTS, 2, ROWS, HEAD), jnp.bfloat16),
            pltpu.VMEM((KV_HEADS, ROWS, HEAD), jnp.bfloat16),
            pltpu.VMEM((HEADS, ROWS, HEAD), jnp.bfloat16),
            pltpu.VMEM((HEADS, ROWS, HEAD), jnp.bfloat16),
            pltpu.VMEM((8, HEAD), jnp.int32),
            pltpu.VMEM((8, HEAD), jnp.int32),
            pltpu.VMEM((WINDOW + 1, ROWS, HEAD), jnp.bfloat16),
            pltpu.VMEM((ROWS, HEAD), jnp.bfloat16),
            pltpu.VMEM((HEADS, ROWS, HEAD), jnp.float32),
            pltpu.VMEM((HEADS, ROWS, HEAD), jnp.float32),
            pltpu.VMEM((HEADS, ROWS, HEAD), jnp.float32),
            dma((6,)),
            dma((4, ROUNDS, STREAMS)),
            dma((4, ROUNDS, STREAMS)),
            dma((KV_HEADS, 2)),
            dma((KV_HEADS, 2)),
            dma((QUERY_COPIES,)),
            dma((QUERY_COPIES,)),
            dma((2,)),
        ],
        compiler_params=pltpu.CompilerParams(
            collective_id=3, has_side_effects=True, vmem_limit_bytes=63 * 2**20
        ),
        name="relayed_attention",
    )(queries, keys, values, modality, query_gain, tower_key_gain, doc_lengths)


def solution(mesh):
    placed = (
        P("section", "ctx", "tp"),
        P("section", "ctx", "tp"),
        P("section", "ctx", "tp"),
        P("section", "ctx"),
        P(None, "tp"),
        P(None, "tp"),
        P("section", None),
    )
    return jax.shard_map(
        body, mesh=mesh, in_specs=placed, out_specs=P("section", "ctx", "tp"), check_vma=False
    )
```

```python
import functools

import jax
import jax.numpy as jnp
from jax import lax
from jax.experimental import pallas as pl
from jax.experimental.pallas import tpu as pltpu
from jax.sharding import PartitionSpec as P

MESH = pl.DeviceIdType.MESH
NT = (((1,), (1,)), ((), ()))
HEAD = 128
ROWS = 192
KV_HEADS = 2
GROUP = 8
HEADS = KV_HEADS * GROUP
BLOCKS = 32
WINDOW = 20
SLOTS = 32
OWN = 31
PER_GROUP = 4
GROUP_KEYS = PER_GROUP * ROWS
KEY_GROUPS = WINDOW // PER_GROUP
BIG = float(1 << 20)
LOG2E = 1.4426950408889634
EXP_SCALE = HEAD ** -0.5 * LOG2E
DIAGONAL = 7

SCHEDULE = (
    (
        0, 32, 64, 161, 193, 225, 322, 354, 386, 483, 515, 547, 611, 644, 676, 708, 805, 837, 869, 933,
        966, 998, 1030, 1127, 1159, 1255, 1288, 1320, 1352, 1449, 1481, 1513, 1545, 1610, 1642, 1674, 1771,
        1803, 1835, 1899, 1932, 1964, 1996, 2028, 2093, 2125, 2157, 2254, 2318, 2382, 2415, 2447, 2576,
        2640, 2737, 2801, 2833, 2898, 2962, 3059, 3123, 3187, 3220, 3284, 3381, 3445, 3509, 3542, 3606,
        3703, 3831, 3928, 4089, 4250, 4411, 4572, 4733, 4894,
    ),
    (
        40, 163, 201, 224, 259, 321, 362, 385, 485, 523, 546, 613, 643, 675, 707, 807, 845, 868, 935, 965,
        997, 1029, 1126, 1167, 1289, 1321, 1344, 1451, 1512, 1537, 1609, 1641, 1673, 1698, 1772, 1802,
        1834, 1934, 1963, 1995, 2062, 2092, 2124, 2156, 2253, 2317, 2374, 2414, 2446, 2577, 2632, 2739,
        2800, 2897, 2961, 3018, 3058, 3122, 3157, 3219, 3283, 3383, 3444, 3501, 3534, 3605, 3702, 3823,
        3872, 3920, 4033, 4088, 4194, 4249, 4306, 4355, 4410, 4516, 4571, 4612, 4677, 4732, 4838, 4893,
        4950, 4999, 5079,
    ),
    (
        3, 41, 165, 197, 261, 320, 361, 384, 487, 519, 545, 615, 642, 683, 706, 803, 844, 867, 909, 964,
        996, 1028, 1125, 1166, 1281, 1442, 1507, 1538, 1614, 1646, 1672, 1710, 1765, 1801, 1833, 1930,
        1994, 2054, 2091, 2123, 2155, 2183, 2252, 2316, 2342, 2406, 2445, 2503, 2570, 2624, 2731, 2785,
        2827, 2901, 2946, 2997, 3052, 3121, 3149, 3214, 3282, 3375, 3443, 3503, 3540, 3604, 3622, 3701,
        3783, 3922, 4080, 4196, 4248, 4292, 4409, 4515, 4570, 4630, 4731, 4759, 4837, 4892, 4910, 5071,
    ),
    (
        5, 37, 167, 199, 263, 366, 430, 481, 521, 544, 641, 685, 705, 802, 843, 866, 963, 995, 1027, 1124,
        1165, 1283, 1443, 1509, 1608, 1638, 1664, 1702, 1768, 1800, 1832, 1863, 1929, 1993, 2022, 2090,
        2122, 2154, 2181, 2251, 2283, 2315, 2340, 2405, 2444, 2571, 2634, 2741, 2784, 2837, 2893, 2916,
        2960, 2989, 3057, 3074, 3106, 3151, 3217, 3281, 3316, 3378, 3442, 3462, 3539, 3603, 3623, 3700,
        3791, 3876, 3912, 4037, 4075, 4115, 4240, 4278, 4359, 4408, 4428, 4523, 4569, 4599, 4686, 4730,
        4751, 4836, 4891, 4916, 5077,
    ),
    (
        7, 39, 206, 270, 358, 422, 520, 684, 704, 801, 833, 865, 962, 1003, 1026, 1123, 1164, 1282, 1446,
        1542, 1607, 1668, 1700, 1770, 1824, 1921, 1992, 2089, 2153, 2250, 2282, 2314, 2404, 2443, 2581,
        2596, 2628, 2733, 2789, 2829, 2895, 2944, 2991, 3060, 3120, 3156, 3209, 3266, 3302, 3377, 3441,
        3463, 3538, 3602, 3620, 3699, 3877, 3914, 4039, 4071, 4118, 4204, 4246, 4268, 4361, 4400, 4439,
        4527, 4568, 4590, 4729, 4754, 4835, 4890, 4915, 5005, 5069,
    ),
    (
        46, 198, 262, 522, 842, 864, 961, 1002, 1025, 1122, 1163, 1286, 1454, 1550, 1761, 1920, 1984, 2088,
        2152, 2242, 2313, 2403, 2573, 2735, 2790, 2831, 2888, 2948, 2996, 3053, 3112, 3139, 3210, 3280,
        3369, 3433, 3461, 3537, 3601, 3619, 3698, 3879, 4044, 4083, 4108, 4203, 4245, 4279, 4366, 4392,
        4436, 4525, 4560, 4591, 4673, 4728, 4757, 4889, 4918, 5004, 5068,
    ),
    (
        38, 960, 1024, 1121, 1294, 2248, 2312, 2410, 2575, 2740, 2836, 3440, 3593, 3697, 3884, 4119, 4720,
        4888, 5003,
    ),
    (
        1120, 2408, 2580, 3600, 4880,
    ),
)
ROUNDS = len(SCHEDULE)


def neighbour(chip, direction):
    x, z = divmod(chip, 8)
    return (
        ((x + 1) % 4) * 8 + z,
        ((x + 3) % 4) * 8 + z,
        chip + 1,
        chip - 1,
        chip - 2,
    )[direction]


def relay_tables():
    slot = [{chip: OWN} for chip in range(BLOCKS)]
    count = [0] * BLOCKS
    spare = [WINDOW] * BLOCKS
    sends = [[[1023] * ROUNDS for _ in range(DIRECTIONS)] for _ in range(BLOCKS)]
    takes = [[[31] * ROUNDS for _ in range(DIRECTIONS)] for _ in range(BLOCKS)]
    ready = [[0] * ROUNDS for _ in range(BLOCKS)]
    for step, entries in enumerate(SCHEDULE):
        known = [dict(held) for held in slot]
        for entry in entries:
            link, block = divmod(entry, 32)
            sender, direction = divmod(link, DIRECTIONS)
            assert direction < 4 or step < FAR_ROUNDS
            target = neighbour(sender, direction)
            if max(0, target - WINDOW) <= block < target:
                place = count[target]
                count[target] += 1
            else:
                place = spare[target]
                spare[target] += 1
            assert place < OWN and block not in slot[target]
            slot[target][block] = place
            sends[sender][direction][step] = known[sender][block] * 32 + place
            takes[target][direction][step] = place
        for chip in range(BLOCKS):
            ready[chip][step] = count[chip] // PER_GROUP
    for chip in range(BLOCKS):
        assert count[chip] == min(chip, WINDOW)
        ready[chip][ROUNDS - 1] = -(-count[chip] // PER_GROUP)
    owners = [[31] * WINDOW for _ in range(BLOCKS)]
    for chip in range(BLOCKS):
        for block, place in slot[chip].items():
            if place < WINDOW:
                owners[chip][place] = block
    return sends, takes, ready, owners, count


def packed(values, bits):
    per = 30 // bits
    return [
        sum(value << (bits * i) for i, value in enumerate(values[at : at + per]))
        for at in range(0, len(values), per)
    ]


def chosen(chip, per_chip):
    result = jnp.int32(per_chip[0])
    for index in range(1, len(per_chip)):
        if per_chip[index] != per_chip[0]:
            result = jnp.where(chip == index, jnp.int32(per_chip[index]), result)
    return result


class Table:
    def __init__(self, chip, per_chip, bits):
        self.bits = bits
        self.per = 30 // bits
        rows = [packed(values, bits) for values in per_chip]
        self.words = [chosen(chip, column) for column in zip(*rows)]

    def at(self, index):
        word = self.words[0]
        for place in range(1, len(self.words)):
            word = jnp.where(index >= place * self.per, self.words[place], word)
        shift = lax.rem(index, self.per) * self.bits
        return lax.shift_right_logical(word, shift) & ((1 << self.bits) - 1)


TILE_HEADS = 4
TILE_ROWS = TILE_HEADS * ROWS
TILES = GROUP // TILE_HEADS
STREAMS = 2 * KV_HEADS
FORWARD_STEP = 0
FORWARD_STEP_2 = 3
FIRST_STEP = 2
SECOND_STEP = 4
CHUNKS = ROUNDS * KV_HEADS + KV_HEADS * (KEY_GROUPS + 1)
QUERY_COPIES = 6
ROUND_HEADS = 4
SPLIT = 4
DIRECTIONS = 5
FAR_ROUNDS = 3


def kernel(
    q_hbm, k_hbm, v_hbm, modality_hbm, q_gain_hbm, k_gain_hbm, docs_hbm, o_ref,
    q_in, k_in, modality, q_gain, k_gain, docs_own,
    kv, key_stage, query_stage, queries, docs_stage, docs_in, key_docs, query_docs,
    peak, total, summed, detour,
    load_sems, link_send, link_recv, whole_send, whole_recv, detour_send, detour_recv, hop_send, hop_recv, query_send, query_recv, docs_sems,
):
    loads = [
        pltpu.make_async_copy(source, target, load_sems.at[index])
        for index, (source, target) in enumerate(
            (
                (k_hbm, k_in), (modality_hbm, modality), (k_gain_hbm, k_gain), (docs_hbm, docs_own),
                (q_gain_hbm, q_gain), (q_hbm, q_in),
            )
        )
    ]
    for load in loads:
        load.start()

    section = lax.axis_index("section")
    chip = lax.axis_index("ctx")
    part = lax.axis_index("tp")
    x, z = chip // 8, lax.rem(chip, 8)
    after = (lax.rem(section + 1, 4), chip, part)
    before = (lax.rem(section + 3, 4), chip, part)
    around = (
        (section, lax.rem(x + 1, 4) * 8 + z, part),
        (section, lax.rem(x + 3, 4) * 8 + z, part),
        (section, x * 8 + jnp.minimum(z + 1, 7), part),
        (section, x * 8 + jnp.maximum(z - 1, 0), part),
        (section, x * 8 + jnp.maximum(z - 2, 0), part),
    )
    further = (section, x * 8 + jnp.minimum(z + 2, 7), part)

    barrier = pltpu.get_barrier_semaphore()
    for device in (after, before, around[0], around[1]):
        pl.semaphore_signal(barrier, inc=1, device_id=device, device_id_type=MESH)
    near = ((around[2], z < 7), (around[3], z > 0))
    if FAR_ROUNDS:
        near += ((around[4], z > 1), (further, z < 6))
    expected = jnp.int32(4)
    for device, exists in near:
        expected += exists.astype(jnp.int32)

        @pl.when(exists)
        def _():
            pl.semaphore_signal(barrier, inc=1, device_id=device, device_id_type=MESH)

    for load in loads[:3]:
        load.wait()
    diagonal = lax.broadcasted_iota(jnp.int32, (ROWS, ROWS), 0) == lax.broadcasted_iota(
        jnp.int32, (ROWS, ROWS), 1
    )
    towers = jnp.sum(
        jnp.where(diagonal, modality[0:1, :].astype(jnp.float32), 0.0), axis=1, keepdims=True
    )
    image = jnp.broadcast_to(towers, (ROWS, HEAD)) > 0.5

    def scaled(values, gain_ref, channels):
        gains = jnp.where(image, gain_ref[1:2, channels], gain_ref[0:1, channels])
        return (values.astype(jnp.float32) * gains).astype(jnp.bfloat16)

    for head in range(KV_HEADS):
        channels = pl.ds(head * HEAD, HEAD)
        key_stage[head] = scaled(k_in[0, :, channels], k_gain, channels)

    pl.semaphore_wait(barrier, expected)

    def hop(head, kind):
        if kind == 0:
            source = key_stage.at[head]
        else:
            source = v_hbm.at[0, :, pl.ds(head * HEAD, HEAD)]
        return pltpu.make_async_remote_copy(
            src_ref=source, dst_ref=kv.at[head, OWN, kind],
            send_sem=hop_send.at[head, kind], recv_sem=hop_recv.at[head, kind],
            device_id=after, device_id_type=MESH,
        )

    for head in range(KV_HEADS):
        for kind in range(2):
            hop(head, kind).start()

    loads[3].wait()
    docs_stage[...] = jnp.zeros_like(docs_stage)
    docs_stage[0:1, 0:16] = docs_own[...]
    docs_copy = pltpu.make_async_remote_copy(
        src_ref=docs_stage, dst_ref=docs_in, send_sem=docs_sems.at[0], recv_sem=docs_sems.at[1],
        device_id=after, device_id_type=MESH,
    )
    docs_copy.start()

    sends, takes, ready, owners, count = relay_tables()
    links = DIRECTIONS if FAR_ROUNDS else 4
    send_tables = [Table(chip, [sends[c][d] for c in range(BLOCKS)], 10) for d in range(links)]
    take_tables = [Table(chip, [takes[c][d] for c in range(BLOCKS)], 5) for d in range(links)]
    ready_table = Table(chip, ready, 3)
    owner_table = Table(chip, owners, 5)
    arrivals = jnp.minimum(chip, WINDOW)
    groups = (arrivals + PER_GROUP - 1) // PER_GROUP

    def link_copy(direction, step, head, kind, source, target):
        if kind is None:
            return pltpu.make_async_remote_copy(
                src_ref=kv.at[head, source], dst_ref=kv.at[head, target],
                send_sem=whole_send.at[direction, step - SPLIT, head],
                recv_sem=whole_recv.at[direction, step - SPLIT, head],
                device_id=around[direction], device_id_type=MESH,
            )
        return pltpu.make_async_remote_copy(
            src_ref=kv.at[head, source, kind], dst_ref=kv.at[head, target, kind],
            send_sem=link_send.at[direction, step, 2 * head + kind],
            recv_sem=link_recv.at[direction, step, 2 * head + kind],
            device_id=around[direction], device_id_type=MESH,
        )

    def start_round(codes, step, head, kind):
        for direction, code in enumerate(codes):
            @pl.when(code != 1023)
            def _():
                link_copy(direction, step, head, kind, code // 32, lax.rem(code, 32)).start()

    def take_round(places, step, head, kind):
        for direction, place in enumerate(places):
            @pl.when(place != 31)
            def _():
                link_copy(direction, step, head, kind, place, place).wait_recv()

    def query_copy(index):
        heads = pl.ds(index * 2, 2)
        return pltpu.make_async_remote_copy(
            src_ref=query_stage.at[heads], dst_ref=queries.at[heads],
            send_sem=query_send.at[index], recv_sem=query_recv.at[index],
            device_id=after, device_id_type=MESH,
        )

    def round_copy(hop_index):
        last_heads = pl.ds(HEADS - ROUND_HEADS, ROUND_HEADS)
        return pltpu.make_async_remote_copy(
            src_ref=query_stage.at[last_heads] if hop_index == 0 else detour.at[hop_index - 1],
            dst_ref=queries.at[last_heads] if hop_index == 2 else detour.at[hop_index],
            send_sem=detour_send.at[hop_index], recv_sem=detour_recv.at[hop_index],
            device_id=before, device_id_type=MESH,
        )

    loads[4].wait()
    loads[5].wait()

    def scale_queries(first_head, last_head):
        for head in range(first_head, last_head):
            channels = pl.ds(head * HEAD, HEAD)
            query_stage[head] = scaled(q_in[0, :, channels], q_gain, channels)

    scale_queries(HEADS - ROUND_HEADS, HEADS)
    round_copy(0).start()
    scale_queries(0, GROUP)
    for index in range(GROUP // 2):
        query_copy(index).start()
    first_codes = [table.at(0) for table in send_tables]
    for head in range(KV_HEADS):
        for kind in range(2):
            hop(head, kind).wait_recv()
            start_round(first_codes, 0, head, kind)
    scale_queries(GROUP, HEADS - ROUND_HEADS)
    for index in range(GROUP // 2, QUERY_COPIES):
        query_copy(index).start()

    def clear(place, carry):
        for head in range(KV_HEADS):
            kv[head, place] = jnp.zeros((2, ROWS, HEAD), jnp.bfloat16)
        return carry

    lax.fori_loop(arrivals, groups * PER_GROUP, clear, 0)

    docs_copy.wait_recv()
    lengths = docs_in[0:1, :].astype(jnp.float32)
    square = (HEAD, HEAD)
    down = lax.broadcasted_iota(jnp.int32, square, 0)
    across = lax.broadcasted_iota(jnp.int32, square, 1)
    column = jnp.sum(jnp.where(down == across, lengths, 0.0), axis=1, keepdims=True)
    first = jnp.sum(jnp.where(down < across, column, 0.0), axis=0, keepdims=True)
    lane = lax.broadcasted_iota(jnp.int32, (1, HEAD), 1)
    last = jnp.where(lane == 15, 1e9, first + lengths)
    first = jnp.where(lane < 16, first, jnp.where(lane == 16, -1e9, 1e9))
    last = jnp.where(lane < 16, last, jnp.where(lane == 16, 0.0, 1e9))
    inner = lax.broadcasted_iota(jnp.int32, (ROWS, HEAD), 0)

    def members(block):
        places = (inner + block * ROWS).astype(jnp.float32)
        return (places >= first) & (places < last)

    def mark(place, carry):
        block = jnp.where(place < arrivals, owner_table.at(place), -1)
        key_docs[place] = jnp.where(members(block), 1.0, 0.0).astype(jnp.bfloat16)
        return carry

    lax.fori_loop(0, groups * PER_GROUP, mark, 0)
    own_members = members(chip)
    key_docs[WINDOW] = jnp.where(own_members, 1.0, 0.0).astype(jnp.bfloat16)
    query_docs[...] = jnp.where(own_members, 0.0, -BIG).astype(jnp.bfloat16)

    def tiles_of(head, keys, values, size, fresh):
        keys, marked = keys
        keys = jnp.concatenate([keys.reshape(size, HEAD), marked.reshape(size, HEAD)], axis=1)
        values = jnp.concatenate(
            [values.reshape(size, HEAD), jnp.ones((size, HEAD), jnp.bfloat16)], axis=1
        )
        marks = jnp.concatenate([query_docs[...]] * TILE_HEADS, axis=0)
        shape = (TILE_HEADS, ROWS, HEAD)

        def rows_of(tile):
            return pl.ds(head * GROUP + tile * TILE_HEADS, TILE_HEADS)

        def score(tile):
            rows = queries[rows_of(tile)].reshape(TILE_ROWS, HEAD)
            rows = jnp.concatenate([rows, marks], axis=1)
            return lax.dot_general(rows, keys, NT, preferred_element_type=jnp.float32)

        scores = {0: score(0)}
        held = {}
        for tile in range(TILES + 1):
            if tile + 1 < TILES:
                scores[tile + 1] = score(tile + 1)
            if tile >= 1:
                weights, shrink = held.pop(tile - 1)
                rows = rows_of(tile - 1)
                mixed = jnp.dot(weights, values, preferred_element_type=jnp.float32)
                if fresh:
                    summed[rows] = mixed[:, :HEAD].reshape(shape)
                    total[rows] = mixed[:, HEAD:].reshape(shape)
                else:
                    summed[rows] = summed[rows] * shrink + mixed[:, :HEAD].reshape(shape)
                    total[rows] = total[rows] * shrink + mixed[:, HEAD:].reshape(shape)
            if tile < TILES:
                rows = rows_of(tile)
                now = scores.pop(tile)
                if fresh:
                    below = lax.broadcasted_iota(jnp.int32, shape[:1] + (ROWS, ROWS), 1)
                    below = below >= lax.broadcasted_iota(jnp.int32, shape[:1] + (ROWS, ROWS), 2)
                    now = jnp.where(below, now.reshape(shape[:1] + (ROWS, ROWS)), -1e30)
                    now = now.reshape(TILE_ROWS, ROWS)
                    new = jnp.broadcast_to(
                        jnp.max(now, axis=1, keepdims=True), (TILE_ROWS, HEAD)
                    )
                    shrink = None
                else:
                    old = peak[rows].reshape(TILE_ROWS, HEAD)
                    new = jnp.maximum(old, jnp.max(now, axis=1, keepdims=True))
                    shrink = jnp.exp2((old - new) * EXP_SCALE).reshape(shape)
                spread = new[:, 0:1] if fresh else jnp.concatenate([new] * (size // HEAD), axis=1)
                weights = jnp.exp2((now - spread) * EXP_SCALE).astype(jnp.bfloat16)
                peak[rows] = new.reshape(shape)
                held[tile] = (weights, shrink)

    def step_body(index, done):
        step, stream = index // KV_HEADS, lax.rem(index, KV_HEADS)
        at = jnp.minimum(step, ROUNDS - 1)
        later = jnp.minimum(step + 1, ROUNDS - 1)

        def exchange(ways, kinds, next_kinds):
            places = [table.at(at) for table in take_tables[:ways]]
            codes = [
                jnp.where(step + 1 < ROUNDS, table.at(later), 1023) for table in send_tables[:ways]
            ]
            for kind in kinds:
                take_round(places, at, stream, kind)
                if len(next_kinds) == len(kinds):
                    start_round(codes, later, stream, kind)
            if len(next_kinds) != len(kinds):
                start_round(codes, later, stream, None)

        @pl.when(step < SPLIT - 1)
        def _():
            exchange(links, (0, 1), (0, 1))

        @pl.when(step == SPLIT - 1)
        def _():
            exchange(4, (0, 1), (None,))

        @pl.when((step >= SPLIT) & (step < ROUNDS))
        def _():
            exchange(4, (None,), (None,))

        @pl.when(index == FORWARD_STEP)
        def _():
            round_copy(0).wait_recv()
            round_copy(1).start()

        @pl.when(index == FORWARD_STEP_2)
        def _():
            round_copy(1).wait_recv()
            round_copy(2).start()

        @pl.when(index == FIRST_STEP)
        def _():
            for copy in range(GROUP // 2):
                query_copy(copy).wait_recv()

        @pl.when(index == SECOND_STEP)
        def _():
            for copy in range(GROUP // 2, QUERY_COPIES):
                query_copy(copy).wait_recv()
            round_copy(2).wait_recv()

        now = jnp.where(step >= ROUNDS, groups, ready_table.at(at))
        past = jnp.where(step == 0, 0, ready_table.at(jnp.maximum(at - 1, 0)))
        past = jnp.where(step >= ROUNDS, groups, past)
        open_first = jnp.where(index >= FIRST_STEP, 1 + now, 0) - done[0]
        open_second = jnp.where(
            index >= SECOND_STEP, 1 + jnp.where(stream == 1, now, past), 0
        ) - done[1]
        pick_first = (open_first > 0) & ((done[0] <= done[1]) | (open_second <= 0))
        pick_second = (open_second > 0) & jnp.logical_not(pick_first)
        head = pick_second.astype(jnp.int32)
        place = jnp.where(pick_second, done[1], done[0])
        some = pick_first | pick_second

        @pl.when(some & (place == 0))
        def _():
            tiles_of(head, (kv[head, OWN, 0], key_docs[WINDOW]), kv[head, OWN, 1], ROWS, True)

        @pl.when(some & (place > 0))
        def _():
            slots = pl.ds((place - 1) * PER_GROUP, PER_GROUP)
            tiles_of(
                head, (kv[head, slots, 0], key_docs[slots]), kv[head, slots, 1], GROUP_KEYS, False
            )

        return (done[0] + pick_first.astype(jnp.int32), done[1] + pick_second.astype(jnp.int32))

    lax.fori_loop(0, CHUNKS, step_body, (jnp.int32(0), jnp.int32(0)))

    for head in range(HEADS):
        o_ref[0, :, pl.ds(head * HEAD, HEAD)] = (summed[head] / total[head]).astype(jnp.bfloat16)

    def drain_split(step, carry):
        for direction, table in enumerate(send_tables):
            code = table.at(step)

            @pl.when(code != 1023)
            def _():
                for head in range(KV_HEADS):
                    for kind in range(2):
                        link_copy(
                            direction, step, head, kind, code // 32, lax.rem(code, 32)
                        ).wait_send()
        return carry

    def drain_whole(step, carry):
        for direction, table in enumerate(send_tables[:4]):
            code = table.at(step)

            @pl.when(code != 1023)
            def _():
                for head in range(KV_HEADS):
                    link_copy(direction, step, head, None, code // 32, lax.rem(code, 32)).wait_send()
        return carry

    lax.fori_loop(0, SPLIT, drain_split, 0)
    lax.fori_loop(SPLIT, ROUNDS, drain_whole, 0)
    for hop_index in range(3):
        round_copy(hop_index).wait_send()
    for head in range(KV_HEADS):
        hop(head, 0).wait_send()
        hop(head, 1).wait_send()
    for index in range(QUERY_COPIES):
        query_copy(index).wait_send()
    docs_copy.wait_send()


def body(queries, keys, values, modality, query_gain, tower_key_gain, doc_lengths):
    vmem = pl.BlockSpec(memory_space=pltpu.VMEM)
    dma = pltpu.SemaphoreType.DMA
    links = DIRECTIONS if FAR_ROUNDS else 4
    attended = pl.pallas_call(
        kernel,
        out_shape=jax.ShapeDtypeStruct(queries.shape, jnp.bfloat16),
        in_specs=[pl.BlockSpec(memory_space=pltpu.HBM)] * 7,
        out_specs=vmem,
        scratch_shapes=[
            pltpu.VMEM(queries.shape, jnp.bfloat16),
            pltpu.VMEM(keys.shape, jnp.bfloat16),
            pltpu.VMEM(modality.shape, jnp.int32),
            pltpu.VMEM(query_gain.shape, jnp.float32),
            pltpu.VMEM(tower_key_gain.shape, jnp.float32),
            pltpu.VMEM(doc_lengths.shape, jnp.int32),
            pltpu.VMEM((KV_HEADS, SLOTS, 2, ROWS, HEAD), jnp.bfloat16),
            pltpu.VMEM((KV_HEADS, ROWS, HEAD), jnp.bfloat16),
            pltpu.VMEM((HEADS, ROWS, HEAD), jnp.bfloat16),
            pltpu.VMEM((HEADS, ROWS, HEAD), jnp.bfloat16),
            pltpu.VMEM((8, HEAD), jnp.int32),
            pltpu.VMEM((8, HEAD), jnp.int32),
            pltpu.VMEM((WINDOW + 1, ROWS, HEAD), jnp.bfloat16),
            pltpu.VMEM((ROWS, HEAD), jnp.bfloat16),
            pltpu.VMEM((HEADS, ROWS, HEAD), jnp.float32),
            pltpu.VMEM((HEADS, ROWS, HEAD), jnp.float32),
            pltpu.VMEM((HEADS, ROWS, HEAD), jnp.float32),
            pltpu.VMEM((2, ROUND_HEADS, ROWS, HEAD), jnp.bfloat16),
            dma((6,)),
            dma((links, SPLIT, STREAMS)),
            dma((links, SPLIT, STREAMS)),
            dma((4, ROUNDS - SPLIT, KV_HEADS)),
            dma((4, ROUNDS - SPLIT, KV_HEADS)),
            dma((3,)),
            dma((3,)),
            dma((KV_HEADS, 2)),
            dma((KV_HEADS, 2)),
            dma((QUERY_COPIES,)),
            dma((QUERY_COPIES,)),
            dma((2,)),
        ],
        compiler_params=pltpu.CompilerParams(
            collective_id=3, has_side_effects=True, vmem_limit_bytes=63 * 2**20
        ),
        name="relayed_attention",
    )(queries, keys, values, modality, query_gain, tower_key_gain, doc_lengths)
    return attended


def solution(mesh):
    placed = (
        P("section", "ctx", "tp"),
        P("section", "ctx", "tp"),
        P("section", "ctx", "tp"),
        P("section", "ctx"),
        P(None, "tp"),
        P(None, "tp"),
        P("section", None),
    )
    return jax.shard_map(
        body, mesh=mesh, in_specs=placed, out_specs=P("section", "ctx", "tp"), check_vma=False
    )
```
